32 devices in a mesh: groups: 2 (over y), pool: 16 (over z, x, core).
Axes of the slice: x: 2, y: 2, z: 4, core: 2. Of those that a mesh axis runs over, the one named last changes fastest.
Arguments:
- queries: bfloat16 [128, 6144], P(('groups', 'pool')), parts along dimension 0, may hold values from -70 to 70
- keys_cache: bfloat16 [128, 192, 1024], P(('groups', 'pool')), parts along dimension 0, may hold values from -3 to 3
- values_cache: bfloat16 [128, 192, 1024], P(('groups', 'pool')), parts along dimension 0, may hold values from -6 to 6
- lengths: int32 [128], P(('groups', 'pool')), parts along dimension 0, may hold values from 1 to 192, 6144 in all
- hidden: bfloat16 [128, 6144], P(('groups', 'pool')), parts along dimension 0, may hold values from -6 to 6
- norm_gain: bfloat16 [6144], replicated, may hold values from 0.25 to 1.75
- expert_ids: int32 [128, 2], P(('groups', 'pool')), parts along dimension 0, may hold values from 0 to 3, all different within a row; in each aligned block of 4 rows (0 to 3, 4 to 7, ...) at most 3 rows name the same one
- gate_weights: bfloat16 [128, 2], P(('groups', 'pool')), parts along dimension 0, may hold values from 0.25 to 1
- w_gate: bfloat16 [6144, 32768], P(None, 'pool'), may hold values from -0.078125 to 0.078125
- w_up: bfloat16 [6144, 32768], P(None, 'pool'), may hold values from -0.078125 to 0.078125
- w_down: bfloat16 [32768, 6144], P('pool'), may hold values from -0.0625 to 0.0625
Outputs:
- context: bfloat16 [128, 6144], P(('groups', 'pool')), parts along dimension 0
- moe_out: bfloat16 [128, 6144], P(('groups', 'pool')), parts along dimension 0
The draws below stay inside these ranges and needn't reach their ends.
There are 2 independent parts, one for each index of `groups`. The reference program is written for one: setup_inputs(seed, part) draws one part's arguments, and reference() takes and returns one part's arrays. A program takes and returns all parts, laid end to end along the dimension named above; an argument that names none is the same for every part. Nothing has to cross between parts.
Inputs may be any that keep to these rules, and one draw needn't show every extreme that they name: `expert_ids`: the two ids of a row differ. Among the 4 rows of one device (aligned blocks of rows), no expert is named by more than 3 rows, and in some blocks one expert is named by exactly 3; every expert is named somewhere. `lengths`: some row has all 192 slots live.
All inputs are finite; a program needn't handle non-finite values. No bound on the sum of `lengths` on one device may be relied on, other than what follows from the above.
Results may differ from the reference program's by a relative error of at most 0.0044.
Values may be sent and summed in bfloat16 or wider, within the bound.
No kernel may reach another device: no remote copies, remote signals or barrier semaphores. Data moves between devices by JAX's collectives and lax.ppermute only.
A program may use at most 192 MiB of HBM per device.

```python
import math
import jax
import jax.numpy as jnp
import numpy as np
from jax import lax

D = 6144
FF = 8192
EXPERTS = 4
TOPK = 2
HEADS = 48
KV_HEADS = 8
HEAD_DIM = 128
ROW_DEV = 4
LEN = 192
CAP = 3
ROWS = 64
N_POOL = 16


def leading_keys(key):
    width = KV_HEADS * HEAD_DIM
    first_keys = jnp.clip(jax.random.normal(jax.random.fold_in(key, 101), (ROWS, width), jnp.float32), -2.5, 2.5)
    nudge_noise = jnp.clip(jax.random.normal(jax.random.fold_in(key, 102), (ROWS, width), jnp.float32), -2.5, 2.5)
    return (first_keys, nudge_noise)


def draw_keys_cache(key, part):
    first_keys, nudge_noise = leading_keys(key)
    key = jax.random.fold_in(key, 3)
    width = KV_HEADS * HEAD_DIM
    rest_keys = jnp.clip(jax.random.normal(key, (ROWS, LEN - 2, width), jnp.float32), -2.5, 2.5)
    second_keys = nudge_noise
    whole = jnp.concatenate([first_keys[:, None, :], second_keys[:, None, :], rest_keys], axis=1)
    return whole.astype(jnp.bfloat16)


def draw_queries(key, part):
    key = jax.random.fold_in(key, 7)
    width = HEADS * HEAD_DIM
    result = jnp.clip(jax.random.normal(key, (ROWS, width), jnp.float32), -6.0, 6.0)
    return result.astype(jnp.bfloat16)


def levels(rng, dims, pieces, least, high):
    gain = 1.0
    for axis_at, blocks in pieces:
        draws = jax.random.uniform(jax.random.fold_in(jax.random.fold_in(rng, 6), axis_at), (blocks,), jnp.float32, least / len(pieces), high / len(pieces))
        gain = gain * jnp.repeat(jnp.exp(draws), dims[axis_at] // blocks).reshape((-1,) + (1,) * (len(dims) - 1 - axis_at))
    return gain


def split_up(amount, total, bound, skew):
    loads = [(1 << 20) // math.isqrt(grade ** skew) + 1 for grade in range(2, amount + 1)]
    rest, given = total - bound - (amount - 1), [1] * (amount - 1)
    while rest > 0:
        free = [i for i in range(amount - 1) if given[i] < bound]
        pool, left = sum([loads[i] for i in free]), rest
        for i in free:
            more = min(bound - given[i], max(1, left * loads[i] // pool), rest)
            given[i] = given[i] + more
            rest = rest - more
    return np.array([bound] + given)


def ragged_sizes(own_key, number_of, total, most, lean):
    if number_of == 2:
        one = jax.random.randint(own_key, (), max(1, total - most), min(most, total - 1) + 1)
        return jnp.stack([one, total - one])
    tallies = jnp.asarray(split_up(number_of, total, most, lean), jnp.int32)
    twos = (number_of - 1) // 2
    giver, sink = tallies[1:1 + 2 * twos:2], tallies[2:2 + 2 * twos:2]
    margin = jnp.minimum(giver - 1, most - sink)
    shifted = jax.random.randint(jax.random.fold_in(own_key, 1), (twos,), 0, 1 << 20) % (margin + 1)
    tallies = tallies.at[1:1 + 2 * twos:2].set(giver - shifted).at[2:2 + 2 * twos:2].set(sink + shifted)
    return tallies[jax.random.permutation(jax.random.fold_in(own_key, 2), number_of)]


def shared_out(key, own, number, rows, number_of, top, most, lean):
    ranking = jax.random.permutation(key, number_of)
    heavy_load, usual = shares(number_of, rows * top, most, lean, True), shares(number_of, rows * top, most, lean, False)
    places = jnp.arange(number_of)

    def named(sizes, turn):
        used = int((sizes > 0).sum())
        fixed = max(1, used // 4)
        shifted = fixed + (places - fixed + turn * (used - fixed)) % max(1, number_of - fixed)
        return jnp.zeros((number_of,), jnp.int32).at[ranking[jnp.where(places < fixed, places, shifted)]].set(jnp.asarray(sizes, jnp.int32))

    sizes = jnp.where(number % 4 == 0, named(heavy_load, number // 4), named(usual, number - number // 4 - 1))
    mixed = jax.random.permutation(jax.random.fold_in(own, 3), number_of)
    source_of, sink = mixed[0:number_of // 2 * 2:2], mixed[1:number_of // 2 * 2:2]
    room = jnp.minimum(sizes[source_of] - 1, most - sizes[sink]) // 2
    room = jnp.where((source_of == ranking[0]) | (sink == ranking[0]) | (sizes[sink] == 0), 0, jnp.maximum(room, 0))
    shifted = jax.random.randint(jax.random.fold_in(own, 4), (number_of // 2,), 0, 1 << 20) % (room + 1)
    sizes = sizes.at[source_of].add(-shifted).at[sink].add(shifted)
    members = jnp.searchsorted(jnp.cumsum(sizes), jnp.arange(rows * top), side="right").astype(jnp.int32)
    table = members.reshape(top, rows).T
    table = table[jax.random.permutation(jax.random.fold_in(own, 1), rows)]
    turn = jax.random.randint(jax.random.fold_in(own, 2), (rows, 1), 0, top)
    return jnp.take_along_axis(table, (jnp.arange(top)[None, :] + turn) % top, axis=1)


def shares(amount, total, bound, skew, full):
    loads = [(1 << 20) // math.isqrt(grade ** skew) + 1 for grade in range(1, amount + 1)]
    largest = bound if full else min(bound, max(-(-total // amount), total * loads[0] // sum(loads)))
    least = 1 if total - largest >= amount - 1 else 0
    counts, rest = [largest] + [least] * (amount - 1), total - largest - least * (amount - 1)
    while rest > 0:
        free = [i for i in range(1, amount) if counts[i] < largest] or [i for i in range(1, amount) if counts[i] < bound]
        mass, remaining = sum([loads[i] for i in free]), rest
        for i in free:
            addition = min(bound - counts[i], max(1, remaining * loads[i] // mass), rest)
            counts[i] = counts[i] + addition
            rest = rest - addition
    return np.array(counts)


def scatter_about(stream_key, dims, deviation, limit, shards=(), held_as=jnp.bfloat16):
    values = jax.random.normal(stream_key, dims, jnp.float32) * deviation
    if len(shards) > 0:
        values = levels(stream_key, dims, shards, -0.22, 0.18) * values
    return jnp.clip(values, min=-limit, max=limit).astype(held_as)


def setup_inputs(seed: int = 0, part: int = 0) -> dict:
    key_of = jax.random.split(jax.random.key(seed), 12)
    own_keys = jax.random.split(jax.random.fold_in(key_of[11], part), 12)
    queries = draw_queries(jax.random.fold_in(jax.random.fold_in(key_of[11], part), 71), part)
    keys_cache = draw_keys_cache(jax.random.fold_in(jax.random.fold_in(key_of[11], part), 71), part)
    values_cache = scatter_about(own_keys[2], (ROWS, LEN, KV_HEADS * HEAD_DIM), 1.0, 6.0, ((0, 16),))
    lengths = ragged_sizes(own_keys[3], ROWS, ROWS * LEN // 2, LEN, 2).astype(jnp.int32)
    hidden = scatter_about(own_keys[4], (ROWS, D), 1.0, 6.0, ((0, 16),))
    norm_gain = jnp.clip(1.0 + 0.15 * jax.random.normal(key_of[5], (D,), jnp.float32), 0.25, 1.75).astype(jnp.bfloat16)
    expert_ids_keys = jax.random.split(jax.random.fold_in(own_keys[6], 1), ROWS // ROW_DEV)
    expert_ids_turns = jax.random.permutation(jax.random.fold_in(own_keys[6], 3), ROWS // ROW_DEV)
    expert_ids = jax.vmap(lambda own, number: shared_out(jax.random.fold_in(own_keys[6], 2), own, number, ROW_DEV, EXPERTS, TOPK, CAP, 2))(expert_ids_keys, expert_ids_turns).reshape((ROWS, TOPK))
    gate_weights = jnp.clip(0.25 + 0.75 * jax.random.uniform(own_keys[7], (ROWS, TOPK), jnp.float32) ** levels(own_keys[7], (ROWS, TOPK), ((0, 16),), -0.2, 0.2), 0.25, 1.0).astype(jnp.bfloat16)
    w_gate = scatter_about(key_of[8], (D, EXPERTS * FF), D ** -0.5, 0.078125, ((1, 16),))
    w_up = scatter_about(key_of[9], (D, EXPERTS * FF), D ** -0.5, 0.078125, ((1, 16),))
    w_down = scatter_about(key_of[10], (EXPERTS * FF, D), FF ** -0.5, 0.0625, ((0, 16),))
    return dict(queries=queries, keys_cache=keys_cache, values_cache=values_cache, lengths=lengths, hidden=hidden, norm_gain=norm_gain, expert_ids=expert_ids, gate_weights=gate_weights, w_gate=w_gate, w_up=w_up, w_down=w_down)


EPS = 1e-05

def normalize(hidden, norm_gain):
    values = hidden.astype(jnp.float32)
    row_scale = lax.rsqrt(lax.optimization_barrier(jnp.mean(values * values, axis=-1, keepdims=True)) + EPS)
    return (values * row_scale * norm_gain.astype(jnp.float32)).astype(jnp.bfloat16)

def expert_ffn(normed, w_gate, w_up, w_down):
    gate_proj = jnp.dot(normed, w_gate, preferred_element_type=jnp.float32)
    up_proj = jnp.dot(normed, w_up, preferred_element_type=jnp.float32)
    active = (jax.nn.silu(gate_proj) * up_proj).astype(jnp.bfloat16)
    return jnp.dot(active, w_down, preferred_element_type=jnp.float32)

def attend(bundle):
    queries, keys_cache, values_cache, lengths = bundle
    row_count = queries.shape[0]
    cache_span = keys_cache.shape[1]
    query_heads = queries.reshape(row_count, KV_HEADS, HEADS // KV_HEADS, HEAD_DIM).astype(jnp.float32)
    key_heads = keys_cache.reshape(row_count, cache_span, KV_HEADS, HEAD_DIM).astype(jnp.float32)
    value_heads = values_cache.reshape(row_count, cache_span, KV_HEADS, HEAD_DIM).astype(jnp.float32)
    scores = jnp.einsum('rkgd,rlkd->rkgl', query_heads, key_heads) * HEAD_DIM ** (-0.5)
    live_mask = jnp.arange(cache_span, dtype=jnp.int32)[None, None, None, :] < lengths[:, None, None, None]
    scores = jnp.where(live_mask, scores, -jnp.inf)
    row_max = lax.optimization_barrier(jnp.max(scores, axis=-1, keepdims=True))
    raised = jnp.exp(scores - row_max)
    row_total = lax.optimization_barrier(jnp.sum(raised, axis=-1, keepdims=True))
    attn_weights = (raised / row_total).astype(jnp.bfloat16).astype(jnp.float32)
    context = jnp.einsum('rkgl,rlkd->rkgd', attn_weights, value_heads)
    return context.reshape(row_count, HEADS * HEAD_DIM).astype(jnp.bfloat16)

def reference(queries, keys_cache, values_cache, lengths, hidden, norm_gain, expert_ids, gate_weights, w_gate, w_up, w_down):
    bundle = (queries.reshape(N_POOL, ROW_DEV, HEADS * HEAD_DIM), keys_cache.reshape(N_POOL, ROW_DEV, LEN, KV_HEADS * HEAD_DIM), values_cache.reshape(N_POOL, ROW_DEV, LEN, KV_HEADS * HEAD_DIM), lengths.reshape(N_POOL, ROW_DEV))
    context = lax.map(attend, bundle).reshape(ROWS, HEADS * HEAD_DIM)
    normed = normalize(hidden, norm_gain)
    picked = expert_ids[:, :, None] == jnp.arange(EXPERTS, dtype=jnp.int32)[None, None, :]
    coefficient = lax.optimization_barrier(jnp.sum(jnp.where(picked, gate_weights[:, :, None].astype(jnp.float32), 0.0), axis=1))

    def one_expert(running, expert_index):
        first_col = expert_index * FF
        gate_cols = lax.dynamic_slice_in_dim(w_gate, first_col, FF, 1)
        up_cols = lax.dynamic_slice_in_dim(w_up, first_col, FF, 1)
        down_rows = lax.dynamic_slice_in_dim(w_down, first_col, FF, 0)
        expert_out = expert_ffn(normed, gate_cols, up_cols, down_rows)
        column = lax.optimization_barrier(jnp.sum(jnp.where(jnp.arange(EXPERTS, dtype=jnp.int32)[None, :] == expert_index, coefficient, 0.0), axis=1))
        return (running + expert_out * column[:, None], None)
    mixture, _ = lax.scan(one_expert, jnp.zeros((ROWS, D), jnp.float32), jnp.arange(EXPERTS, dtype=jnp.int32))
    moe_out = (hidden.astype(jnp.float32) + mixture).astype(jnp.bfloat16)
    return (context, moe_out)
```

```python
import functools

import jax
import jax.numpy as jnp
from jax import lax
from jax.experimental import pallas as pl
from jax.experimental.pallas import tpu as pltpu
from jax.sharding import PartitionSpec as P

EXPERTS = 4
HEADS = 48
KV_HEADS = 8
HEAD_DIM = 128
EPS = 1e-05
MIB = 1 << 20


def norm_kernel(hidden_ref, gain_ref, normed_ref):
    values = hidden_ref[...].astype(jnp.float32)
    row_scale = lax.rsqrt(jnp.mean(values * values, axis=-1, keepdims=True) + EPS)
    normed_ref[...] = (values * row_scale * gain_ref[...].astype(jnp.float32)).astype(jnp.bfloat16)


def normalize(hidden, norm_gain):
    return pl.pallas_call(
        norm_kernel,
        out_shape=jax.ShapeDtypeStruct(hidden.shape, jnp.bfloat16),
        compiler_params=pltpu.CompilerParams(vmem_limit_bytes=8 * MIB),
    )(hidden, norm_gain.reshape(1, -1))


def ffn_kernel(
    depth, width, x_ref, gate_hbm, up_hbm, down_hbm, keep_ref, send_ref,
    gate_buf, up_buf, down_buf, gate_sum, up_sum, active, gate_sem, up_sem, down_sem,
):
    ring = gate_buf.shape[0]
    down_ring = down_buf.shape[0]
    steps = gate_hbm.shape[0] // depth
    down_steps = down_hbm.shape[1] // width
    half = keep_ref.shape[0]

    def gate_copy(step, slot):
        rows = pl.ds(pl.multiple_of(step * depth, depth), depth)
        return pltpu.make_async_copy(gate_hbm.at[rows, :], gate_buf.at[slot], gate_sem.at[slot])

    def up_copy(step, slot):
        rows = pl.ds(pl.multiple_of(step * depth, depth), depth)
        return pltpu.make_async_copy(up_hbm.at[rows, :], up_buf.at[slot], up_sem.at[slot])

    def down_copy(step, slot):
        columns = pl.ds(pl.multiple_of(step * width, width), width)
        return pltpu.make_async_copy(
            down_hbm.at[:, columns], down_buf.at[slot], down_sem.at[slot]
        )

    for step in range(min(ring, steps)):
        gate_copy(step, step).start()
        up_copy(step, step).start()
    for step in range(min(down_ring, down_steps)):
        down_copy(step, step).start()
    gate_sum[...] = jnp.zeros_like(gate_sum)
    up_sum[...] = jnp.zeros_like(up_sum)

    @pl.loop(0, steps)
    def _(step):
        slot = lax.rem(step, ring)
        block = x_ref[:, pl.ds(pl.multiple_of(step * depth, depth), depth)]
        gate_copy(step, slot).wait()
        gate_sum[...] += jnp.dot(block, gate_buf[slot], preferred_element_type=jnp.float32)
        up_copy(step, slot).wait()
        up_sum[...] += jnp.dot(block, up_buf[slot], preferred_element_type=jnp.float32)

        @pl.when(step + ring < steps)
        def _():
            gate_copy(step + ring, slot).start()
            up_copy(step + ring, slot).start()

    gate_proj = gate_sum[...]
    active[...] = (gate_proj / (1.0 + jnp.exp(-gate_proj)) * up_sum[...]).astype(jnp.bfloat16)

    @pl.loop(0, down_steps)
    def _(step):
        slot = lax.rem(step, down_ring)
        columns = pl.ds(pl.multiple_of(step * width, width), width)
        down_copy(step, slot).wait()
        out = jnp.dot(active[...], down_buf[slot], preferred_element_type=jnp.float32)
        keep_ref[:, columns] = out[:half]
        send_ref[:, columns] = out[half:].astype(jnp.bfloat16)

        @pl.when(step + down_ring < down_steps)
        def _():
            down_copy(step + down_ring, slot).start()


def expert_ffn(x, w_gate, w_up, w_down):
    rows, model_width = x.shape
    units = w_gate.shape[1]
    depth = 1024
    width = 1024
    ring = 3
    down_ring = 3
    hbm = pl.BlockSpec(memory_space=pl.ANY)
    vmem = pl.BlockSpec(memory_space=pltpu.VMEM)
    return pl.pallas_call(
        functools.partial(ffn_kernel, depth, width),
        out_shape=(
            jax.ShapeDtypeStruct((rows // 2, model_width), jnp.float32),
            jax.ShapeDtypeStruct((rows // 2, model_width), jnp.bfloat16),
        ),
        in_specs=[vmem, hbm, hbm, hbm],
        out_specs=(vmem, vmem),
        scratch_shapes=[
            pltpu.VMEM((ring, depth, units), jnp.bfloat16),
            pltpu.VMEM((ring, depth, units), jnp.bfloat16),
            pltpu.VMEM((down_ring, units, width), jnp.bfloat16),
            pltpu.VMEM((rows, units), jnp.float32),
            pltpu.VMEM((rows, units), jnp.float32),
            pltpu.VMEM((rows, units), jnp.bfloat16),
            pltpu.SemaphoreType.DMA((ring,)),
            pltpu.SemaphoreType.DMA((ring,)),
            pltpu.SemaphoreType.DMA((down_ring,)),
        ],
        compiler_params=pltpu.CompilerParams(vmem_limit_bytes=50 * MIB),
        cost_estimate=pl.CostEstimate(
            flops=6 * rows * model_width * units,
            bytes_accessed=6 * model_width * units,
            transcendentals=rows * units,
        ),
    )(x, w_gate, w_up, w_down)


def attend(queries, keys_cache, values_cache, lengths):
    row_count = queries.shape[0]
    cache_span = keys_cache.shape[1]
    query_heads = queries.reshape(row_count, KV_HEADS, HEADS // KV_HEADS, HEAD_DIM)
    key_heads = keys_cache.reshape(row_count, cache_span, KV_HEADS, HEAD_DIM)
    value_heads = values_cache.reshape(row_count, cache_span, KV_HEADS, HEAD_DIM)
    scores = jnp.einsum(
        "rkgd,rlkd->rkgl", query_heads, key_heads, preferred_element_type=jnp.float32
    ) * HEAD_DIM ** (-0.5)
    live_mask = (
        jnp.arange(cache_span, dtype=jnp.int32)[None, None, None, :] < lengths[:, None, None, None]
    )
    scores = jnp.where(live_mask, scores, -jnp.inf)
    row_max = jnp.max(scores, axis=-1, keepdims=True)
    raised = jnp.exp(scores - row_max)
    row_total = jnp.sum(raised, axis=-1, keepdims=True)
    attn_weights = (raised / row_total).astype(jnp.bfloat16)
    context = jnp.einsum(
        "rkgl,rlkd->rkgd", attn_weights, value_heads, preferred_element_type=jnp.float32
    )
    return context.reshape(row_count, HEADS * HEAD_DIM).astype(jnp.bfloat16)


def local(
    queries,
    keys_cache,
    values_cache,
    lengths,
    hidden,
    norm_gain,
    expert_ids,
    gate_weights,
    w_gate,
    w_up,
    w_down,
):
    devices = lax.axis_size("pool")
    group_size = devices // EXPERTS
    own_rows = hidden.shape[0]

    def swap(value, distance):
        return lax.ppermute(value, "pool", [(i, i ^ distance) for i in range(devices)])

    near = []
    distance = 1
    while distance < group_size:
        near.append(distance)
        distance *= 2

    normed = normalize(hidden, norm_gain)
    x = jnp.concatenate(
        [normed] + [swap(normed, k * group_size) for k in range(1, EXPERTS)], axis=0
    )
    for distance in reversed(near):
        x = jnp.concatenate([x, swap(x, distance)], axis=0)

    keep, send = expert_ffn(x, w_gate, w_up, w_down)
    for at, distance in enumerate(near):
        total = keep + swap(send, distance).astype(jnp.float32)
        if at + 1 < len(near):
            half = total.shape[0] // 2
            keep, send = total[:half], total[half:].astype(jnp.bfloat16)

    own_expert = lax.axis_index("pool") // group_size
    mixture = jnp.zeros(hidden.shape, jnp.float32)
    for k in range(EXPERTS):
        block = total[k * own_rows : (k + 1) * own_rows]
        if k > 0:
            block = swap(block.astype(jnp.bfloat16), k * group_size).astype(jnp.float32)
        named = expert_ids == (own_expert ^ k)
        coefficient = jnp.sum(
            jnp.where(named, gate_weights.astype(jnp.float32), 0.0), axis=1, keepdims=True
        )
        mixture = mixture + coefficient * block
    moe_out = (hidden.astype(jnp.float32) + mixture).astype(jnp.bfloat16)
    context = attend(queries, keys_cache, values_cache, lengths)
    return (context, moe_out)


def solution(mesh):
    return jax.shard_map(
        local,
        mesh=mesh,
        in_specs=(
            P(("groups", "pool"), None),
            P(("groups", "pool"), None, None),
            P(("groups", "pool"), None, None),
            P(("groups", "pool")),
            P(("groups", "pool"), None),
            P(),
            P(("groups", "pool"), None),
            P(("groups", "pool"), None),
            P(None, "pool"),
            P(None, "pool"),
            P("pool", None),
        ),
        out_specs=(P(("groups", "pool"), None), P(("groups", "pool"), None)),
        check_vma=False,
    )
```

```python
import functools

import jax
import jax.numpy as jnp
from jax import lax
from jax.experimental import pallas as pl
from jax.experimental.pallas import tpu as pltpu
from jax.sharding import PartitionSpec as P

EXPERTS = 4
HEADS = 48
KV_HEADS = 8
HEAD_DIM = 128
EPS = 1e-05
MIB = 1 << 20
HBM = pl.BlockSpec(memory_space=pl.ANY)
VMEM = pl.BlockSpec(memory_space=pltpu.VMEM)
SMEM = pl.BlockSpec(memory_space=pltpu.SMEM)


def norm_kernel(hidden_hbm, gain_hbm, normed_ref, hidden_ref, gain_ref, sems):
    hidden_copy = pltpu.make_async_copy(hidden_hbm, hidden_ref, sems.at[0])
    gain_copy = pltpu.make_async_copy(gain_hbm, gain_ref, sems.at[1])
    hidden_copy.start()
    gain_copy.start()
    hidden_copy.wait()
    values = hidden_ref[...].astype(jnp.float32)
    row_scale = lax.rsqrt(jnp.mean(values * values, axis=-1, keepdims=True) + EPS)
    gain_copy.wait()
    gain = gain_ref[...].astype(jnp.float32).reshape(1, -1)
    normed_ref[...] = (values * row_scale * gain).astype(jnp.bfloat16)


def normalize(hidden, norm_gain):
    return pl.pallas_call(
        norm_kernel,
        out_shape=jax.ShapeDtypeStruct(hidden.shape, jnp.bfloat16),
        in_specs=[HBM, HBM],
        out_specs=VMEM,
        scratch_shapes=[
            pltpu.VMEM(hidden.shape, hidden.dtype),
            pltpu.VMEM(norm_gain.shape, norm_gain.dtype),
            pltpu.SemaphoreType.DMA((2,)),
        ],
        compiler_params=pltpu.CompilerParams(vmem_limit_bytes=60 * MIB),
    )(hidden, norm_gain)


def merge_kernel(count, *refs):
    merged_ref = refs[-1]
    merged_ref[...] = jnp.concatenate([ref[...] for ref in refs[:count]], axis=0)


def merge(blocks, after):
    rows = sum(block.shape[0] for block in blocks)
    return pl.pallas_call(
        functools.partial(merge_kernel, len(blocks)),
        in_specs=[VMEM] * (len(blocks) + len(after)),
        out_specs=VMEM,
        out_shape=jax.ShapeDtypeStruct((rows, blocks[0].shape[1]), blocks[0].dtype),
        compiler_params=pltpu.CompilerParams(vmem_limit_bytes=4 * MIB),
    )(*blocks, *after)


def prefetch_kernel(firsts, *refs):
    count = len(firsts)
    sources, targets, sems = refs[:count], refs[count + 1 : 2 * count + 1], refs[-1]
    copies = [
        pltpu.make_async_copy(source.at[pl.ds(first, target.shape[0]), :], target, sems.at[i])
        for i, (source, first, target) in enumerate(zip(sources, firsts, targets))
    ]
    for copy in copies:
        copy.start()
    for copy in copies:
        copy.wait()


def prefetch(parts, after, limit):
    total = sum(count * weights.shape[1] for weights, _, count in parts)
    return pl.pallas_call(
        functools.partial(prefetch_kernel, tuple(first for _, first, _ in parts)),
        out_shape=tuple(
            pltpu.VMEM((count, weights.shape[1]), weights.dtype) for weights, _, count in parts
        ),
        in_specs=[HBM] * len(parts) + [HBM],
        out_specs=(VMEM,) * len(parts),
        scratch_shapes=[pltpu.SemaphoreType.DMA((len(parts),))],
        compiler_params=pltpu.CompilerParams(vmem_limit_bytes=limit * MIB),
        cost_estimate=pl.CostEstimate(flops=0, bytes_accessed=2 * total, transcendentals=0),
    )(*[weights for weights, _, _ in parts], after)


def ffn_kernel(piece_count, gate_count, up_depth, width, *refs):
    pieces, refs = refs[:piece_count], refs[piece_count:]
    gates, refs = refs[:gate_count], refs[gate_count:]
    up_hbm, down_hbm, keep_ref, send_ref = refs[:4]
    up_buf, down_buf, x, gate_sum, up_sum, active, up_sem, down_sem = refs[4:]
    ring = up_buf.shape[0]
    down_ring = down_buf.shape[0]
    up_steps = up_hbm.shape[0] // up_depth
    down_steps = down_hbm.shape[1] // width
    half = keep_ref.shape[0]

    def up_rows(step):
        return pl.ds(pl.multiple_of(step * up_depth, up_depth), up_depth)

    def up_copy(step, slot):
        return pltpu.make_async_copy(
            up_hbm.at[up_rows(step), :], up_buf.at[slot], up_sem.at[slot]
        )

    def down_copy(step, slot):
        columns = pl.ds(pl.multiple_of(step * width, width), width)
        return pltpu.make_async_copy(
            down_hbm.at[:, columns], down_buf.at[slot], down_sem.at[slot]
        )

    for step in range(min(ring, up_steps)):
        up_copy(step, step).start()
    for step in range(min(down_ring, down_steps)):
        down_copy(step, step).start()
    at = 0
    for piece in pieces:
        x[at : at + piece.shape[0], :] = piece[...]
        at += piece.shape[0]
    gate_sum[...] = jnp.zeros_like(gate_sum)
    up_sum[...] = jnp.zeros_like(up_sum)

    depth = 1024
    offset = 0
    for part in gates:

        @pl.loop(0, part.shape[0] // depth)
        def _(step):
            rows = pl.ds(pl.multiple_of(step * depth, depth), depth)
            columns = pl.ds(pl.multiple_of(offset + step * depth, depth), depth)
            gate_sum[...] += jnp.dot(
                x[:, columns], part[rows, :], preferred_element_type=jnp.float32
            )

        offset += part.shape[0]

    @pl.loop(0, up_steps)
    def _(step):
        slot = lax.rem(step, ring)
        up_copy(step, slot).wait()
        up_sum[...] += jnp.dot(
            x[:, up_rows(step)], up_buf[slot], preferred_element_type=jnp.float32
        )

        @pl.when(step + ring < up_steps)
        def _():
            up_copy(step + ring, slot).start()

    gate_proj = gate_sum[...]
    active[...] = (gate_proj / (1.0 + jnp.exp(-gate_proj)) * up_sum[...]).astype(jnp.bfloat16)

    @pl.loop(0, down_steps)
    def _(step):
        slot = lax.rem(step, down_ring)
        columns = pl.ds(pl.multiple_of(step * width, width), width)
        down_copy(step, slot).wait()
        out = jnp.dot(active[...], down_buf[slot], preferred_element_type=jnp.float32)
        keep_ref[:, columns] = out[:half]
        send_ref[:, columns] = out[half:].astype(jnp.bfloat16)

        @pl.when(step + down_ring < down_steps)
        def _():
            down_copy(step + down_ring, slot).start()


def expert_ffn(pieces, gates, w_up, w_down):
    rows = sum(piece.shape[0] for piece in pieces)
    model_width, units = w_up.shape
    up_depth, ring = 512, 4
    width, down_ring = 512, 6
    return pl.pallas_call(
        functools.partial(ffn_kernel, len(pieces), len(gates), up_depth, width),
        out_shape=(
            jax.ShapeDtypeStruct((rows // 2, model_width), jnp.float32),
            jax.ShapeDtypeStruct((rows // 2, model_width), jnp.bfloat16),
        ),
        in_specs=[VMEM] * (len(pieces) + len(gates)) + [HBM, HBM],
        out_specs=(VMEM, VMEM),
        scratch_shapes=[
            pltpu.VMEM((ring, up_depth, units), jnp.bfloat16),
            pltpu.VMEM((down_ring, units, width), jnp.bfloat16),
            pltpu.VMEM((rows, model_width), jnp.bfloat16),
            pltpu.VMEM((rows, units), jnp.float32),
            pltpu.VMEM((rows, units), jnp.float32),
            pltpu.VMEM((rows, units), jnp.bfloat16),
            pltpu.SemaphoreType.DMA((ring,)),
            pltpu.SemaphoreType.DMA((down_ring,)),
        ],
        compiler_params=pltpu.CompilerParams(vmem_limit_bytes=24 * MIB),
        cost_estimate=pl.CostEstimate(
            flops=6 * rows * model_width * units,
            bytes_accessed=6 * model_width * units,
            transcendentals=rows * units,
        ),
    )(*pieces, *gates, w_up, w_down)


def split_kernel(keep_ref, received_ref, *refs):
    kept_ref, sent_refs = refs[-1], refs[-2]
    total = keep_ref[...] + received_ref[...].astype(jnp.float32)
    at = kept_ref.shape[0]
    kept_ref[...] = total[:at]
    sent_refs[...] = total[at:].astype(jnp.bfloat16)


def split_in_two(keep, received):
    half, width = keep.shape[0] // 2, keep.shape[1]
    sent, kept = pl.pallas_call(
        split_kernel,
        in_specs=[VMEM, VMEM],
        out_specs=(VMEM, VMEM),
        out_shape=(
            jax.ShapeDtypeStruct((half, width), jnp.bfloat16),
            jax.ShapeDtypeStruct((half, width), jnp.float32),
        ),
        compiler_params=pltpu.CompilerParams(vmem_limit_bytes=16 * MIB),
    )(keep, received)
    return kept, sent


def split_by_expert_kernel(keep_ref, received_ref, after, kept_ref, *sent_refs):
    total = keep_ref[...] + received_ref[...].astype(jnp.float32)
    rows = kept_ref.shape[0]
    kept_ref[...] = total[:rows]
    for k, sent_ref in enumerate(sent_refs):
        sent_ref[...] = total[(k + 1) * rows : (k + 2) * rows].astype(jnp.bfloat16)


def split_by_expert(keep, received, after):
    rows, width = keep.shape[0] // EXPERTS, keep.shape[1]
    return pl.pallas_call(
        split_by_expert_kernel,
        in_specs=[VMEM, VMEM, HBM],
        out_specs=(VMEM,) * EXPERTS,
        out_shape=(jax.ShapeDtypeStruct((rows, width), jnp.float32),)
        + (jax.ShapeDtypeStruct((rows, width), jnp.bfloat16),) * (EXPERTS - 1),
        compiler_params=pltpu.CompilerParams(vmem_limit_bytes=16 * MIB),
    )(keep, received, after)


def finish_kernel(hidden_ref, coefficient_ref, kept_ref, *refs):
    received_refs, out_ref = refs[:-1], refs[-1]
    mixture = coefficient_ref[:, 0:1] * kept_ref[...]
    for k, received_ref in enumerate(received_refs):
        mixture += coefficient_ref[:, k + 1 : k + 2] * received_ref[...].astype(jnp.float32)
    out_ref[...] = (hidden_ref[...].astype(jnp.float32) + mixture).astype(jnp.bfloat16)


def finish(hidden, coefficient, kept, received):
    return pl.pallas_call(
        finish_kernel,
        in_specs=[VMEM] * (3 + len(received)),
        out_specs=VMEM,
        out_shape=jax.ShapeDtypeStruct(hidden.shape, jnp.bfloat16),
        compiler_params=pltpu.CompilerParams(vmem_limit_bytes=8 * MIB),
    )(hidden, coefficient, kept, *received)


def attend_kernel(
    lengths_ref, queries_ref, keys_ref, values_ref, context_ref, query_heads, context_heads
):
    row_count, cache_span, width = keys_ref.shape
    group = HEADS // KV_HEADS
    for h in range(HEADS):
        query_heads[:, h, :] = queries_ref[:, h * HEAD_DIM : (h + 1) * HEAD_DIM].astype(jnp.float32)
    own_head = lax.broadcasted_iota(jnp.int32, (HEADS, width), 0) // group
    lane_head = lax.broadcasted_iota(jnp.int32, (HEADS, width), 1) // HEAD_DIM
    on_diagonal = own_head == lane_head
    slot = lax.broadcasted_iota(jnp.int32, (HEADS, cache_span), 1)
    for r in range(row_count):
        spread = jnp.where(on_diagonal, jnp.concatenate([query_heads[r]] * KV_HEADS, axis=1), 0.0)
        scores = lax.dot_general(
            spread.astype(jnp.bfloat16), keys_ref[r], (((1,), (1,)), ((), ())),
            preferred_element_type=jnp.float32,
        ) * HEAD_DIM ** (-0.5)
        scores = jnp.where(slot < lengths_ref[r], scores, -jnp.inf)
        raised = jnp.exp(scores - jnp.max(scores, axis=-1, keepdims=True))
        weights = (raised / jnp.sum(raised, axis=-1, keepdims=True)).astype(jnp.bfloat16)
        mixed = jnp.dot(weights, values_ref[r], preferred_element_type=jnp.float32)
        mixed = jnp.where(on_diagonal, mixed, 0.0)
        folded = mixed[:, :HEAD_DIM]
        for j in range(1, KV_HEADS):
            folded = folded + mixed[:, j * HEAD_DIM : (j + 1) * HEAD_DIM]
        context_heads[r] = folded
    for h in range(HEADS):
        context_ref[:, h * HEAD_DIM : (h + 1) * HEAD_DIM] = context_heads[:, h, :].astype(jnp.bfloat16)


def attend(queries, keys_cache, values_cache, lengths):
    row_count, cache_span, width = keys_cache.shape
    vmem = pl.BlockSpec(memory_space=pltpu.VMEM)
    return pl.pallas_call(
        attend_kernel,
        out_shape=jax.ShapeDtypeStruct(queries.shape, jnp.bfloat16),
        in_specs=[pl.BlockSpec(memory_space=pltpu.SMEM), vmem, vmem, vmem],
        out_specs=vmem,
        scratch_shapes=[
            pltpu.VMEM((row_count, HEADS, HEAD_DIM), jnp.float32),
            pltpu.VMEM((row_count, HEADS, HEAD_DIM), jnp.float32),
        ],
        compiler_params=pltpu.CompilerParams(vmem_limit_bytes=8 * MIB),
        cost_estimate=pl.CostEstimate(
            flops=4 * row_count * HEADS * cache_span * width,
            bytes_accessed=4 * row_count * cache_span * width,
            transcendentals=row_count * HEADS * cache_span,
        ),
    )(lengths, queries, keys_cache, values_cache)


def local(
    queries,
    keys_cache,
    values_cache,
    lengths,
    hidden,
    norm_gain,
    expert_ids,
    gate_weights,
    w_gate,
    w_up,
    w_down,
):
    devices = lax.axis_size("pool")
    group_size = devices // EXPERTS
    own_rows = hidden.shape[0]

    def swap(value, distance):
        return lax.ppermute(value, "pool", [(i, i ^ distance) for i in range(devices)])

    near = []
    distance = 1
    while distance < group_size:
        near.append(distance)
        distance *= 2

    depth = w_gate.shape[0]
    normed = normalize(hidden, norm_gain)
    (gate_low,) = prefetch([(w_gate, 0, depth // 2)], normed, 36)
    blocks = [normed] + [swap(normed, k * group_size) for k in range(1, EXPERTS)]
    x = merge(blocks, [gate_low])
    (gate_high,) = prefetch([(w_gate, depth // 2, depth // 2)], x, 36)
    pieces, after = [x], [gate_high]
    for distance in reversed(near):
        arrived = [swap(piece, distance) for piece in pieces]
        if after:
            arrived[0] = merge(arrived[:1], after)
        pieces, after = pieces + arrived, []
    keep, send = expert_ffn(pieces, (gate_low, gate_high), w_up, w_down)

    context = attend(queries, keys_cache, values_cache, lengths)
    own_expert = lax.axis_index("pool") // group_size
    order = own_expert ^ jnp.arange(EXPERTS, dtype=jnp.int32)
    named = expert_ids[:, :, None] == order[None, None, :]
    coefficient = jnp.sum(
        jnp.where(named, gate_weights.astype(jnp.float32)[:, :, None], 0.0), axis=1
    )
    for distance in near[:-1]:
        keep, send = split_in_two(keep, swap(send, distance))
    kept, *sent = split_by_expert(keep, swap(send, near[-1]), context)
    received = [swap(block, (k + 1) * group_size) for k, block in enumerate(sent)]
    moe_out = finish(hidden, coefficient, kept, received)
    return (context, moe_out)


def solution(mesh):
    return jax.shard_map(
        local,
        mesh=mesh,
        in_specs=(
            P(("groups", "pool"), None),
            P(("groups", "pool"), None, None),
            P(("groups", "pool"), None, None),
            P(("groups", "pool")),
            P(("groups", "pool"), None),
            P(),
            P(("groups", "pool"), None),
            P(("groups", "pool"), None),
            P(None, "pool"),
            P(None, "pool"),
            P("pool", None),
        ),
        out_specs=(P(("groups", "pool"), None), P(("groups", "pool"), None)),
        check_vma=False,
    )
```

```python
import functools

import jax
import jax.numpy as jnp
from jax import lax
from jax.experimental import pallas as pl
from jax.experimental.pallas import tpu as pltpu
from jax.sharding import PartitionSpec as P

EXPERTS = 4
HEADS = 48
KV_HEADS = 8
HEAD_DIM = 128
EPS = 1e-05
MIB = 1 << 20
HBM = pl.BlockSpec(memory_space=pl.ANY)
VMEM = pl.BlockSpec(memory_space=pltpu.VMEM)
SMEM = pl.BlockSpec(memory_space=pltpu.SMEM)


def norm_kernel(hidden_hbm, gain_hbm, normed_ref, hidden_ref, gain_ref, sems):
    hidden_copy = pltpu.make_async_copy(hidden_hbm, hidden_ref, sems.at[0])
    gain_copy = pltpu.make_async_copy(gain_hbm, gain_ref, sems.at[1])
    hidden_copy.start()
    gain_copy.start()
    hidden_copy.wait()
    values = hidden_ref[...].astype(jnp.float32)
    row_scale = lax.rsqrt(jnp.mean(values * values, axis=-1, keepdims=True) + EPS)
    gain_copy.wait()
    gain = gain_ref[...].astype(jnp.float32).reshape(1, -1)
    normed_ref[...] = (values * row_scale * gain).astype(jnp.bfloat16)


def normalize(hidden, norm_gain):
    return pl.pallas_call(
        norm_kernel,
        out_shape=jax.ShapeDtypeStruct(hidden.shape, jnp.bfloat16),
        in_specs=[HBM, HBM],
        out_specs=VMEM,
        scratch_shapes=[
            pltpu.VMEM(hidden.shape, hidden.dtype),
            pltpu.VMEM(norm_gain.shape, norm_gain.dtype),
            pltpu.SemaphoreType.DMA((2,)),
        ],
        compiler_params=pltpu.CompilerParams(vmem_limit_bytes=60 * MIB),
    )(hidden, norm_gain)


def merge_kernel(count, *refs):
    merged_ref = refs[-1]
    merged_ref[...] = jnp.concatenate([ref[...] for ref in refs[:count]], axis=0)


def merge(blocks, after):
    rows = sum(block.shape[0] for block in blocks)
    return pl.pallas_call(
        functools.partial(merge_kernel, len(blocks)),
        in_specs=[VMEM] * (len(blocks) + len(after)),
        out_specs=VMEM,
        out_shape=jax.ShapeDtypeStruct((rows, blocks[0].shape[1]), blocks[0].dtype),
        compiler_params=pltpu.CompilerParams(vmem_limit_bytes=4 * MIB),
    )(*blocks, *after)


def prefetch_kernel(firsts, *refs):
    count = len(firsts)
    sources, targets, sems = refs[:count], refs[count + 1 : 2 * count + 1], refs[-1]
    copies = [
        pltpu.make_async_copy(source.at[pl.ds(first, target.shape[0]), :], target, sems.at[i])
        for i, (source, first, target) in enumerate(zip(sources, firsts, targets))
    ]
    for copy in copies:
        copy.start()
    for copy in copies:
        copy.wait()


def prefetch(parts, after, limit):
    total = sum(count * weights.shape[1] for weights, _, count in parts)
    return pl.pallas_call(
        functools.partial(prefetch_kernel, tuple(first for _, first, _ in parts)),
        out_shape=tuple(
            pltpu.VMEM((count, weights.shape[1]), weights.dtype) for weights, _, count in parts
        ),
        in_specs=[HBM] * len(parts) + [HBM],
        out_specs=(VMEM,) * len(parts),
        scratch_shapes=[pltpu.SemaphoreType.DMA((len(parts),))],
        compiler_params=pltpu.CompilerParams(vmem_limit_bytes=limit * MIB),
        cost_estimate=pl.CostEstimate(flops=0, bytes_accessed=2 * total, transcendentals=0),
    )(*[weights for weights, _, _ in parts], after)


def ffn_kernel(piece_count, gate_count, *refs):
    pieces, refs = refs[:piece_count], refs[piece_count:]
    gates, refs = refs[:gate_count], refs[gate_count:]
    up_hbm, down_hbm, keep_ref, send_ref = refs[:4]
    chunks, x, gate_sum, up_sum, active, sems = refs[4:]
    ring, depth, width = chunks.shape
    up_steps = up_hbm.shape[0] // depth
    down_parts = down_hbm.shape[0] // depth
    down_steps = down_parts * (down_hbm.shape[1] // width)
    half = keep_ref.shape[0]

    def block(index, size):
        return pl.ds(pl.multiple_of(index * size, size), size)

    def up_copy(step):
        slot = lax.rem(step, ring)
        return pltpu.make_async_copy(
            up_hbm.at[block(step, depth), :], chunks.at[slot], sems.at[slot]
        )

    def down_copy(step):
        slot = lax.rem(step + up_steps, ring)
        part = down_hbm.at[
            block(lax.rem(step, down_parts), depth), block(lax.div(step, down_parts), width)
        ]
        return pltpu.make_async_copy(part, chunks.at[slot], sems.at[slot])

    def issue(step):
        @pl.when(step < up_steps)
        def _():
            up_copy(step).start()

        @pl.when((step >= up_steps) & (step < up_steps + down_steps))
        def _():
            down_copy(step - up_steps).start()

    for step in range(ring):
        issue(jnp.int32(step))
    at = 0
    for piece in pieces:
        x[at : at + piece.shape[0], :] = piece[...]
        at += piece.shape[0]
    gate_sum[...] = jnp.zeros_like(gate_sum)
    up_sum[...] = jnp.zeros_like(up_sum)

    gate_depth = 1024
    offset = 0
    for part in gates:

        @pl.loop(0, part.shape[0] // gate_depth)
        def _(step):
            columns = pl.ds(pl.multiple_of(offset + step * gate_depth, gate_depth), gate_depth)
            gate_sum[...] += jnp.dot(
                x[:, columns], part[block(step, gate_depth), :], preferred_element_type=jnp.float32
            )

        offset += part.shape[0]

    @pl.loop(0, up_steps)
    def _(step):
        up_copy(step).wait()
        up_sum[...] += jnp.dot(
            x[:, block(step, depth)], chunks[lax.rem(step, ring)], preferred_element_type=jnp.float32
        )
        issue(step + ring)

    gate_proj = gate_sum[...]
    active[...] = (gate_proj / (1.0 + jnp.exp(-gate_proj)) * up_sum[...]).astype(jnp.bfloat16)

    @pl.loop(0, down_steps // down_parts)
    def _(column):
        for part in range(down_parts):
            step = column * down_parts + part
            down_copy(step).wait()
            out = jnp.dot(
                active[:, part * depth : (part + 1) * depth],
                chunks[lax.rem(step + up_steps, ring)],
                preferred_element_type=jnp.float32,
            )
            if part > 0:
                out += gate_sum[...]
            if part + 1 < down_parts:
                gate_sum[...] = out
            else:
                keep_ref[:, block(column, width)] = out[:half]
                send_ref[:, block(column, width)] = out[half:].astype(jnp.bfloat16)
            issue(step + up_steps + ring)


def expert_ffn(pieces, gates, w_up, w_down):
    rows = sum(piece.shape[0] for piece in pieces)
    model_width, units = w_up.shape
    ring, depth = 10, min(512, units)
    return pl.pallas_call(
        functools.partial(ffn_kernel, len(pieces), len(gates)),
        out_shape=(
            jax.ShapeDtypeStruct((rows // 2, model_width), jnp.float32),
            jax.ShapeDtypeStruct((rows // 2, model_width), jnp.bfloat16),
        ),
        in_specs=[VMEM] * (len(pieces) + len(gates)) + [HBM, HBM],
        out_specs=(VMEM, VMEM),
        scratch_shapes=[
            pltpu.VMEM((ring, depth, units), jnp.bfloat16),
            pltpu.VMEM((rows, model_width), jnp.bfloat16),
            pltpu.VMEM((rows, units), jnp.float32),
            pltpu.VMEM((rows, units), jnp.float32),
            pltpu.VMEM((rows, units), jnp.bfloat16),
            pltpu.SemaphoreType.DMA((ring,)),
        ],
        compiler_params=pltpu.CompilerParams(vmem_limit_bytes=24 * MIB),
        cost_estimate=pl.CostEstimate(
            flops=6 * rows * model_width * units,
            bytes_accessed=6 * model_width * units,
            transcendentals=rows * units,
        ),
    )(*pieces, *gates, w_up, w_down)


def split_kernel(keep_ref, received_ref, *refs):
    kept_ref, sent_refs = refs[-1], refs[-2]
    total = keep_ref[...] + received_ref[...].astype(jnp.float32)
    at = kept_ref.shape[0]
    kept_ref[...] = total[:at]
    sent_refs[...] = total[at:].astype(jnp.bfloat16)


def split_in_two(keep, received):
    half, width = keep.shape[0] // 2, keep.shape[1]
    sent, kept = pl.pallas_call(
        split_kernel,
        in_specs=[VMEM, VMEM],
        out_specs=(VMEM, VMEM),
        out_shape=(
            jax.ShapeDtypeStruct((half, width), jnp.bfloat16),
            jax.ShapeDtypeStruct((half, width), jnp.float32),
        ),
        compiler_params=pltpu.CompilerParams(vmem_limit_bytes=16 * MIB),
    )(keep, received)
    return kept, sent


def split_by_expert_kernel(keep_ref, received_ref, token_ref, kept_ref, *sent_refs):
    total = keep_ref[...] + received_ref[...].astype(jnp.float32)
    rows = kept_ref.shape[0]
    kept_ref[...] = total[:rows]
    for k, sent_ref in enumerate(sent_refs):
        sent_ref[...] = total[(k + 1) * rows : (k + 2) * rows].astype(jnp.bfloat16)


def split_by_expert(keep, received, token):
    rows, width = keep.shape[0] // EXPERTS, keep.shape[1]
    return pl.pallas_call(
        split_by_expert_kernel,
        in_specs=[VMEM, VMEM, VMEM],
        out_specs=(VMEM,) * EXPERTS,
        out_shape=(jax.ShapeDtypeStruct((rows, width), jnp.float32),)
        + (jax.ShapeDtypeStruct((rows, width), jnp.bfloat16),) * (EXPERTS - 1),
        compiler_params=pltpu.CompilerParams(vmem_limit_bytes=16 * MIB),
    )(keep, received, token)


def finish_kernel(hidden_ref, coefficient_ref, kept_ref, *refs):
    received_refs, out_ref = refs[:-1], refs[-1]
    mixture = coefficient_ref[:, 0:1] * kept_ref[...]
    for k, received_ref in enumerate(received_refs):
        mixture += coefficient_ref[:, k + 1 : k + 2] * received_ref[...].astype(jnp.float32)
    out_ref[...] = (hidden_ref[...].astype(jnp.float32) + mixture).astype(jnp.bfloat16)


def finish(hidden, coefficient, kept, received):
    return pl.pallas_call(
        finish_kernel,
        in_specs=[VMEM] * (3 + len(received)),
        out_specs=VMEM,
        out_shape=jax.ShapeDtypeStruct(hidden.shape, jnp.bfloat16),
        compiler_params=pltpu.CompilerParams(vmem_limit_bytes=8 * MIB),
    )(hidden, coefficient, kept, *received)


def attend_kernel(
    lengths_ref, queries_ref, keys_ref, values_ref, context_ref, token_ref,
    query_heads, context_heads,
):
    token_ref[...] = jnp.zeros_like(token_ref)
    row_count, cache_span, width = keys_ref.shape
    group = HEADS // KV_HEADS
    for h in range(HEADS):
        query_heads[:, h, :] = queries_ref[:, h * HEAD_DIM : (h + 1) * HEAD_DIM].astype(jnp.float32)
    own_head = lax.broadcasted_iota(jnp.int32, (HEADS, width), 0) // group
    lane_head = lax.broadcasted_iota(jnp.int32, (HEADS, width), 1) // HEAD_DIM
    on_diagonal = own_head == lane_head
    slot = lax.broadcasted_iota(jnp.int32, (HEADS, cache_span), 1)
    for r in range(row_count):
        spread = jnp.where(on_diagonal, jnp.concatenate([query_heads[r]] * KV_HEADS, axis=1), 0.0)
        scores = lax.dot_general(
            spread.astype(jnp.bfloat16), keys_ref[r], (((1,), (1,)), ((), ())),
            preferred_element_type=jnp.float32,
        ) * HEAD_DIM ** (-0.5)
        scores = jnp.where(slot < lengths_ref[r], scores, -jnp.inf)
        raised = jnp.exp(scores - jnp.max(scores, axis=-1, keepdims=True))
        weights = (raised / jnp.sum(raised, axis=-1, keepdims=True)).astype(jnp.bfloat16)
        mixed = jnp.dot(weights, values_ref[r], preferred_element_type=jnp.float32)
        mixed = jnp.where(on_diagonal, mixed, 0.0)
        folded = mixed[:, :HEAD_DIM]
        for j in range(1, KV_HEADS):
            folded = folded + mixed[:, j * HEAD_DIM : (j + 1) * HEAD_DIM]
        context_heads[r] = folded
    for h in range(HEADS):
        context_ref[:, h * HEAD_DIM : (h + 1) * HEAD_DIM] = context_heads[:, h, :].astype(jnp.bfloat16)


def attend(queries, keys_cache, values_cache, lengths):
    row_count, cache_span, width = keys_cache.shape
    return pl.pallas_call(
        attend_kernel,
        out_shape=(
            jax.ShapeDtypeStruct(queries.shape, jnp.bfloat16),
            jax.ShapeDtypeStruct((8, 128), jnp.float32),
        ),
        in_specs=[SMEM, VMEM, VMEM, VMEM],
        out_specs=(VMEM, VMEM),
        scratch_shapes=[
            pltpu.VMEM((row_count, HEADS, HEAD_DIM), jnp.float32),
            pltpu.VMEM((row_count, HEADS, HEAD_DIM), jnp.float32),
        ],
        compiler_params=pltpu.CompilerParams(vmem_limit_bytes=8 * MIB),
        cost_estimate=pl.CostEstimate(
            flops=4 * row_count * HEADS * cache_span * width,
            bytes_accessed=4 * row_count * cache_span * width,
            transcendentals=row_count * HEADS * cache_span,
        ),
    )(lengths, queries, keys_cache, values_cache)


def local(
    queries,
    keys_cache,
    values_cache,
    lengths,
    hidden,
    norm_gain,
    expert_ids,
    gate_weights,
    w_gate,
    w_up,
    w_down,
):
    devices = lax.axis_size("pool")
    group_size = devices // EXPERTS
    own_rows = hidden.shape[0]

    def swap(value, distance):
        return lax.ppermute(value, "pool", [(i, i ^ distance) for i in range(devices)])

    near = []
    distance = 1
    while distance < group_size:
        near.append(distance)
        distance *= 2

    normed = normalize(hidden, norm_gain)
    first = prefetch([(w_gate, 0, 3072)], normed, 36)
    blocks = [normed] + [swap(normed, k * group_size) for k in range(1, EXPERTS)]
    x = merge(blocks, [first[-1]])
    second = prefetch([(w_gate, 3072, 3072)], x, 36)
    pieces, after = [x], [second[-1]]
    for distance in reversed(near):
        arrived = [swap(piece, distance) for piece in pieces]
        if after:
            arrived[0] = merge(arrived[:1], after)
        pieces, after = pieces + arrived, []
    keep, send = expert_ffn(pieces, first + second, w_up, w_down)

    context, token = attend(queries, keys_cache, values_cache, lengths)
    own_expert = lax.axis_index("pool") // group_size
    order = own_expert ^ jnp.arange(EXPERTS, dtype=jnp.int32)
    named = expert_ids[:, :, None] == order[None, None, :]
    coefficient = jnp.sum(
        jnp.where(named, gate_weights.astype(jnp.float32)[:, :, None], 0.0), axis=1
    )
    for distance in near[:-1]:
        keep, send = split_in_two(keep, swap(send, distance))
    kept, *sent = split_by_expert(keep, swap(send, near[-1]), token)
    received = [swap(block, (k + 1) * group_size) for k, block in enumerate(sent)]
    moe_out = finish(hidden, coefficient, kept, received)
    return (context, moe_out)


def solution(mesh):
    return jax.shard_map(
        local,
        mesh=mesh,
        in_specs=(
            P(("groups", "pool"), None),
            P(("groups", "pool"), None, None),
            P(("groups", "pool"), None, None),
            P(("groups", "pool")),
            P(("groups", "pool"), None),
            P(),
            P(("groups", "pool"), None),
            P(("groups", "pool"), None),
            P(None, "pool"),
            P(None, "pool"),
            P("pool", None),
        ),
        out_specs=(P(("groups", "pool"), None), P(("groups", "pool"), None)),
        check_vma=False,
    )
```

```python
import functools

import jax
import jax.numpy as jnp
from jax import lax
from jax.experimental import pallas as pl
from jax.experimental.pallas import tpu as pltpu
from jax.sharding import PartitionSpec as P

EXPERTS = 4
HEADS = 48
KV_HEADS = 8
HEAD_DIM = 128
EPS = 1e-05
MIB = 1 << 20
HBM = pl.BlockSpec(memory_space=pl.ANY)
VMEM = pl.BlockSpec(memory_space=pltpu.VMEM)
SMEM = pl.BlockSpec(memory_space=pltpu.SMEM)


def norm_kernel(hidden_hbm, gain_hbm, normed_ref, hidden_ref, gain_ref, sems):
    hidden_copy = pltpu.make_async_copy(hidden_hbm, hidden_ref, sems.at[0])
    gain_copy = pltpu.make_async_copy(gain_hbm, gain_ref, sems.at[1])
    hidden_copy.start()
    gain_copy.start()
    hidden_copy.wait()
    values = hidden_ref[...].astype(jnp.float32)
    row_scale = lax.rsqrt(jnp.mean(values * values, axis=-1, keepdims=True) + EPS)
    gain_copy.wait()
    gain = gain_ref[...].astype(jnp.float32).reshape(1, -1)
    normed_ref[...] = (values * row_scale * gain).astype(jnp.bfloat16)


def normalize(hidden, norm_gain):
    return pl.pallas_call(
        norm_kernel,
        out_shape=pltpu.VMEM(hidden.shape, jnp.bfloat16),
        in_specs=[HBM, HBM],
        out_specs=VMEM,
        scratch_shapes=[
            pltpu.VMEM(hidden.shape, hidden.dtype),
            pltpu.VMEM(norm_gain.shape, norm_gain.dtype),
            pltpu.SemaphoreType.DMA((2,)),
        ],
        compiler_params=pltpu.CompilerParams(vmem_limit_bytes=60 * MIB),
    )(hidden, norm_gain)


def merge_kernel(count, *refs):
    merged_ref = refs[-1]
    merged_ref[...] = jnp.concatenate([ref[...] for ref in refs[:count]], axis=0)


def merge(blocks, after):
    rows = sum(block.shape[0] for block in blocks)
    return pl.pallas_call(
        functools.partial(merge_kernel, len(blocks)),
        in_specs=[VMEM] * (len(blocks) + len(after)),
        out_specs=VMEM,
        out_shape=jax.ShapeDtypeStruct((rows, blocks[0].shape[1]), blocks[0].dtype),
        compiler_params=pltpu.CompilerParams(vmem_limit_bytes=4 * MIB),
    )(*blocks, *after)


def prefetch_kernel(firsts, *refs):
    count = len(firsts)
    sources, targets, sems = refs[:count], refs[count + 1 : 2 * count + 1], refs[-1]
    copies = [
        pltpu.make_async_copy(source.at[pl.ds(first, target.shape[0]), :], target, sems.at[i])
        for i, (source, first, target) in enumerate(zip(sources, firsts, targets))
    ]
    for copy in copies:
        copy.start()
    for copy in copies:
        copy.wait()


def prefetch(parts, after, limit):
    total = sum(count * weights.shape[1] for weights, _, count in parts)
    return pl.pallas_call(
        functools.partial(prefetch_kernel, tuple(first for _, first, _ in parts)),
        out_shape=tuple(
            pltpu.VMEM((count, weights.shape[1]), weights.dtype) for weights, _, count in parts
        ),
        in_specs=[HBM] * len(parts) + [HBM],
        out_specs=(VMEM,) * len(parts),
        scratch_shapes=[pltpu.SemaphoreType.DMA((len(parts),))],
        compiler_params=pltpu.CompilerParams(vmem_limit_bytes=limit * MIB),
        cost_estimate=pl.CostEstimate(flops=0, bytes_accessed=2 * total, transcendentals=0),
    )(*[weights for weights, _, _ in parts], after)


def ffn_kernel(piece_count, gate_count, *refs):
    pieces, refs = refs[:piece_count], refs[piece_count:]
    gates, refs = refs[:gate_count], refs[gate_count:]
    up_hbm, down_hbm, keep_ref, send_ref = refs[:4]
    chunks, x, gate_sum, up_sum, active, sems = refs[4:]
    ring, depth, width = chunks.shape
    up_steps = up_hbm.shape[0] // depth
    down_parts = down_hbm.shape[0] // depth
    down_steps = down_parts * (down_hbm.shape[1] // width)
    half = keep_ref.shape[0]

    def block(index, size):
        return pl.ds(pl.multiple_of(index * size, size), size)

    def up_copy(step):
        slot = lax.rem(step, ring)
        return pltpu.make_async_copy(
            up_hbm.at[block(step, depth), :], chunks.at[slot], sems.at[slot]
        )

    def down_copy(step):
        slot = lax.rem(step + up_steps, ring)
        part = down_hbm.at[
            block(lax.rem(step, down_parts), depth), block(lax.div(step, down_parts), width)
        ]
        return pltpu.make_async_copy(part, chunks.at[slot], sems.at[slot])

    def issue(step):
        @pl.when(step < up_steps)
        def _():
            up_copy(step).start()

        @pl.when((step >= up_steps) & (step < up_steps + down_steps))
        def _():
            down_copy(step - up_steps).start()

    for step in range(ring):
        issue(jnp.int32(step))
    at = 0
    for piece in pieces:
        x[at : at + piece.shape[0], :] = piece[...]
        at += piece.shape[0]
    gate_sum[...] = jnp.zeros_like(gate_sum)
    up_sum[...] = jnp.zeros_like(up_sum)

    gate_depth = 1024
    offset = 0
    for part in gates:

        @pl.loop(0, part.shape[0] // gate_depth)
        def _(step):
            columns = pl.ds(pl.multiple_of(offset + step * gate_depth, gate_depth), gate_depth)
            gate_sum[...] += jnp.dot(
                x[:, columns], part[block(step, gate_depth), :], preferred_element_type=jnp.float32
            )

        offset += part.shape[0]

    @pl.loop(0, up_steps)
    def _(step):
        up_copy(step).wait()
        up_sum[...] += jnp.dot(
            x[:, block(step, depth)], chunks[lax.rem(step, ring)], preferred_element_type=jnp.float32
        )
        issue(step + ring)

    gate_proj = gate_sum[...]
    active[...] = (gate_proj / (1.0 + jnp.exp(-gate_proj)) * up_sum[...]).astype(jnp.bfloat16)

    @pl.loop(0, down_steps // down_parts)
    def _(column):
        for part in range(down_parts):
            step = column * down_parts + part
            down_copy(step).wait()
            out = jnp.dot(
                active[:, part * depth : (part + 1) * depth],
                chunks[lax.rem(step + up_steps, ring)],
                preferred_element_type=jnp.float32,
            )
            if part > 0:
                out += gate_sum[...]
            if part + 1 < down_parts:
                gate_sum[...] = out
            else:
                keep_ref[:, block(column, width)] = out[:half]
                send_ref[:, block(column, width)] = out[half:].astype(jnp.bfloat16)
            issue(step + up_steps + ring)


def expert_ffn(pieces, gates, w_up, w_down):
    rows = sum(piece.shape[0] for piece in pieces)
    model_width, units = w_up.shape
    ring, depth = 10, min(512, units)
    return pl.pallas_call(
        functools.partial(ffn_kernel, len(pieces), len(gates)),
        out_shape=(
            jax.ShapeDtypeStruct((rows // 2, model_width), jnp.float32),
            jax.ShapeDtypeStruct((rows // 2, model_width), jnp.bfloat16),
        ),
        in_specs=[VMEM] * (len(pieces) + len(gates)) + [HBM, HBM],
        out_specs=(VMEM, VMEM),
        scratch_shapes=[
            pltpu.VMEM((ring, depth, units), jnp.bfloat16),
            pltpu.VMEM((rows, model_width), jnp.bfloat16),
            pltpu.VMEM((rows, units), jnp.float32),
            pltpu.VMEM((rows, units), jnp.float32),
            pltpu.VMEM((rows, units), jnp.bfloat16),
            pltpu.SemaphoreType.DMA((ring,)),
        ],
        compiler_params=pltpu.CompilerParams(vmem_limit_bytes=24 * MIB),
        cost_estimate=pl.CostEstimate(
            flops=6 * rows * model_width * units,
            bytes_accessed=6 * model_width * units,
            transcendentals=rows * units,
        ),
    )(*pieces, *gates, w_up, w_down)


def split_kernel(keep_ref, received_ref, *refs):
    kept_ref, sent_refs = refs[-1], refs[-2]
    total = keep_ref[...] + received_ref[...].astype(jnp.float32)
    at = kept_ref.shape[0]
    kept_ref[...] = total[:at]
    sent_refs[...] = total[at:].astype(jnp.bfloat16)


def split_in_two(keep, received):
    half, width = keep.shape[0] // 2, keep.shape[1]
    sent, kept = pl.pallas_call(
        split_kernel,
        in_specs=[VMEM, VMEM],
        out_specs=(VMEM, VMEM),
        out_shape=(
            jax.ShapeDtypeStruct((half, width), jnp.bfloat16),
            jax.ShapeDtypeStruct((half, width), jnp.float32),
        ),
        compiler_params=pltpu.CompilerParams(vmem_limit_bytes=16 * MIB),
    )(keep, received)
    return kept, sent


def split_by_expert_kernel(keep_ref, received_ref, token_ref, kept_ref, *sent_refs):
    total = keep_ref[...] + received_ref[...].astype(jnp.float32)
    rows = kept_ref.shape[0]
    kept_ref[...] = total[:rows]
    for k, sent_ref in enumerate(sent_refs):
        sent_ref[...] = total[(k + 1) * rows : (k + 2) * rows].astype(jnp.bfloat16)


def split_by_expert(keep, received, token):
    rows, width = keep.shape[0] // EXPERTS, keep.shape[1]
    return pl.pallas_call(
        split_by_expert_kernel,
        in_specs=[VMEM, VMEM, VMEM],
        out_specs=(VMEM,) * EXPERTS,
        out_shape=(jax.ShapeDtypeStruct((rows, width), jnp.float32),)
        + (jax.ShapeDtypeStruct((rows, width), jnp.bfloat16),) * (EXPERTS - 1),
        compiler_params=pltpu.CompilerParams(vmem_limit_bytes=16 * MIB),
    )(keep, received, token)


def finish_kernel(hidden_ref, coefficient_ref, kept_ref, *refs):
    received_refs, out_ref = refs[:-1], refs[-1]
    mixture = coefficient_ref[:, 0:1] * kept_ref[...]
    for k, received_ref in enumerate(received_refs):
        mixture += coefficient_ref[:, k + 1 : k + 2] * received_ref[...].astype(jnp.float32)
    out_ref[...] = (hidden_ref[...].astype(jnp.float32) + mixture).astype(jnp.bfloat16)


def finish(hidden, coefficient, kept, received):
    return pl.pallas_call(
        finish_kernel,
        in_specs=[VMEM] * (3 + len(received)),
        out_specs=VMEM,
        out_shape=jax.ShapeDtypeStruct(hidden.shape, jnp.bfloat16),
        compiler_params=pltpu.CompilerParams(vmem_limit_bytes=8 * MIB),
    )(hidden, coefficient, kept, *received)


def attend_kernel(
    lengths_ref, queries_ref, keys_ref, values_ref, context_ref, token_ref,
    query_heads, context_heads,
):
    token_ref[...] = jnp.zeros_like(token_ref)
    row_count, cache_span, width = keys_ref.shape
    group = HEADS // KV_HEADS
    for h in range(HEADS):
        query_heads[:, h, :] = queries_ref[:, h * HEAD_DIM : (h + 1) * HEAD_DIM].astype(jnp.float32)
    own_head = lax.broadcasted_iota(jnp.int32, (HEADS, width), 0) // group
    lane_head = lax.broadcasted_iota(jnp.int32, (HEADS, width), 1) // HEAD_DIM
    on_diagonal = own_head == lane_head
    slot = lax.broadcasted_iota(jnp.int32, (HEADS, cache_span), 1)
    for r in range(row_count):
        spread = jnp.where(on_diagonal, jnp.concatenate([query_heads[r]] * KV_HEADS, axis=1), 0.0)
        scores = lax.dot_general(
            spread.astype(jnp.bfloat16), keys_ref[r], (((1,), (1,)), ((), ())),
            preferred_element_type=jnp.float32,
        ) * HEAD_DIM ** (-0.5)
        scores = jnp.where(slot < lengths_ref[r], scores, -jnp.inf)
        raised = jnp.exp(scores - jnp.max(scores, axis=-1, keepdims=True))
        weights = (raised / jnp.sum(raised, axis=-1, keepdims=True)).astype(jnp.bfloat16)
        mixed = jnp.dot(weights, values_ref[r], preferred_element_type=jnp.float32)
        mixed = jnp.where(on_diagonal, mixed, 0.0)
        folded = mixed[:, :HEAD_DIM]
        for j in range(1, KV_HEADS):
            folded = folded + mixed[:, j * HEAD_DIM : (j + 1) * HEAD_DIM]
        context_heads[r] = folded
    for h in range(HEADS):
        context_ref[:, h * HEAD_DIM : (h + 1) * HEAD_DIM] = context_heads[:, h, :].astype(jnp.bfloat16)


def attend(queries, keys_cache, values_cache, lengths):
    row_count, cache_span, width = keys_cache.shape
    return pl.pallas_call(
        attend_kernel,
        out_shape=(
            jax.ShapeDtypeStruct(queries.shape, jnp.bfloat16),
            jax.ShapeDtypeStruct((8, 128), jnp.float32),
        ),
        in_specs=[SMEM, VMEM, VMEM, VMEM],
        out_specs=(VMEM, VMEM),
        scratch_shapes=[
            pltpu.VMEM((row_count, HEADS, HEAD_DIM), jnp.float32),
            pltpu.VMEM((row_count, HEADS, HEAD_DIM), jnp.float32),
        ],
        compiler_params=pltpu.CompilerParams(vmem_limit_bytes=8 * MIB),
        cost_estimate=pl.CostEstimate(
            flops=4 * row_count * HEADS * cache_span * width,
            bytes_accessed=4 * row_count * cache_span * width,
            transcendentals=row_count * HEADS * cache_span,
        ),
    )(lengths, queries, keys_cache, values_cache)


def local(
    queries,
    keys_cache,
    values_cache,
    lengths,
    hidden,
    norm_gain,
    expert_ids,
    gate_weights,
    w_gate,
    w_up,
    w_down,
):
    devices = lax.axis_size("pool")
    group_size = devices // EXPERTS
    own_rows = hidden.shape[0]

    def swap(value, distance):
        return lax.ppermute(value, "pool", [(i, i ^ distance) for i in range(devices)])

    near = []
    distance = 1
    while distance < group_size:
        near.append(distance)
        distance *= 2

    normed = normalize(hidden, norm_gain)
    first = prefetch([(w_gate, 0, 3072)], normed, 36)
    blocks = [normed] + [swap(normed, k * group_size) for k in range(1, EXPERTS)]
    x = merge(blocks, [first[-1]])
    second = prefetch([(w_gate, 3072, 3072)], x, 36)
    pieces, after = [x], [second[-1]]
    for distance in reversed(near):
        arrived = [swap(piece, distance) for piece in pieces]
        if after:
            arrived[0] = merge(arrived[:1], after)
        pieces, after = pieces + arrived, []
    keep, send = expert_ffn(pieces, first + second, w_up, w_down)

    context, token = attend(queries, keys_cache, values_cache, lengths)
    own_expert = lax.axis_index("pool") // group_size
    order = own_expert ^ jnp.arange(EXPERTS, dtype=jnp.int32)
    named = expert_ids[:, :, None] == order[None, None, :]
    coefficient = jnp.sum(
        jnp.where(named, gate_weights.astype(jnp.float32)[:, :, None], 0.0), axis=1
    )
    for distance in near[:-1]:
        keep, send = split_in_two(keep, swap(send, distance))
    kept, *sent = split_by_expert(keep, swap(send, near[-1]), token)
    received = [swap(block, (k + 1) * group_size) for k, block in enumerate(sent)]
    moe_out = finish(hidden, coefficient, kept, received)
    return (context, moe_out)


def solution(mesh):
    return jax.shard_map(
        local,
        mesh=mesh,
        in_specs=(
            P(("groups", "pool"), None),
            P(("groups", "pool"), None, None),
            P(("groups", "pool"), None, None),
            P(("groups", "pool")),
            P(("groups", "pool"), None),
            P(),
            P(("groups", "pool"), None),
            P(("groups", "pool"), None),
            P(None, "pool"),
            P(None, "pool"),
            P("pool", None),
        ),
        out_specs=(P(("groups", "pool"), None), P(("groups", "pool"), None)),
        check_vma=False,
    )
```

```python
import functools

import jax
import jax.numpy as jnp
from jax import lax
from jax.experimental import pallas as pl
from jax.experimental.pallas import tpu as pltpu
from jax.sharding import PartitionSpec as P

EXPERTS = 4
HEADS = 48
KV_HEADS = 8
HEAD_DIM = 128
EPS = 1e-05
MIB = 1 << 20
HBM = pl.BlockSpec(memory_space=pl.ANY)
VMEM = pl.BlockSpec(memory_space=pltpu.VMEM)
SMEM = pl.BlockSpec(memory_space=pltpu.SMEM)


def norm_kernel(hidden_hbm, gain_hbm, normed_ref, hidden_ref, gain_ref, sems):
    hidden_copy = pltpu.make_async_copy(hidden_hbm, hidden_ref, sems.at[0])
    gain_copy = pltpu.make_async_copy(gain_hbm, gain_ref, sems.at[1])
    hidden_copy.start()
    gain_copy.start()
    hidden_copy.wait()
    values = hidden_ref[...].astype(jnp.float32)
    row_scale = lax.rsqrt(jnp.mean(values * values, axis=-1, keepdims=True) + EPS)
    gain_copy.wait()
    gain = gain_ref[...].astype(jnp.float32).reshape(1, -1)
    normed_ref[...] = (values * row_scale * gain).astype(jnp.bfloat16)


def normalize(hidden, norm_gain):
    return pl.pallas_call(
        norm_kernel,
        out_shape=pltpu.VMEM(hidden.shape, jnp.bfloat16),
        in_specs=[HBM, HBM],
        out_specs=VMEM,
        scratch_shapes=[
            pltpu.VMEM(hidden.shape, hidden.dtype),
            pltpu.VMEM(norm_gain.shape, norm_gain.dtype),
            pltpu.SemaphoreType.DMA((2,)),
        ],
        compiler_params=pltpu.CompilerParams(vmem_limit_bytes=60 * MIB),
    )(hidden, norm_gain)


def merge_kernel(count, *refs):
    merged_ref = refs[-1]
    merged_ref[...] = jnp.concatenate([ref[...] for ref in refs[:count]], axis=0)


def merge(blocks, after):
    rows = sum(block.shape[0] for block in blocks)
    return pl.pallas_call(
        functools.partial(merge_kernel, len(blocks)),
        in_specs=[VMEM] * (len(blocks) + len(after)),
        out_specs=VMEM,
        out_shape=jax.ShapeDtypeStruct((rows, blocks[0].shape[1]), blocks[0].dtype),
        compiler_params=pltpu.CompilerParams(vmem_limit_bytes=4 * MIB),
    )(*blocks, *after)


def prefetch_kernel(firsts, *refs):
    count = len(firsts)
    sources, targets, sems = refs[:count], refs[count + 1 : 2 * count + 1], refs[-1]
    copies = [
        pltpu.make_async_copy(source.at[pl.ds(first, target.shape[0]), :], target, sems.at[i])
        for i, (source, first, target) in enumerate(zip(sources, firsts, targets))
    ]
    for copy in copies:
        copy.start()
    for copy in copies:
        copy.wait()


def prefetch(parts, after, limit):
    total = sum(count * weights.shape[1] for weights, _, count in parts)
    return pl.pallas_call(
        functools.partial(prefetch_kernel, tuple(first for _, first, _ in parts)),
        out_shape=tuple(
            pltpu.VMEM((count, weights.shape[1]), weights.dtype) for weights, _, count in parts
        ),
        in_specs=[HBM] * len(parts) + [HBM],
        out_specs=(VMEM,) * len(parts),
        scratch_shapes=[pltpu.SemaphoreType.DMA((len(parts),))],
        compiler_params=pltpu.CompilerParams(vmem_limit_bytes=limit * MIB),
        cost_estimate=pl.CostEstimate(flops=0, bytes_accessed=2 * total, transcendentals=0),
    )(*[weights for weights, _, _ in parts], after)


def ffn_kernel(piece_count, gate_count, *refs):
    pieces, refs = refs[:piece_count], refs[piece_count:]
    gates, refs = refs[:gate_count], refs[gate_count:]
    up_hbm, down_hbm, keep_ref, send_ref = refs[:4]
    chunks, x, gate_sum, up_sum, active, sems = refs[4:]
    ring, depth, width = chunks.shape
    up_steps = up_hbm.shape[0] // depth
    down_parts = down_hbm.shape[0] // depth
    down_steps = down_parts * (down_hbm.shape[1] // width)
    half = keep_ref.shape[0]

    def block(index, size):
        return pl.ds(pl.multiple_of(index * size, size), size)

    def up_copy(step):
        slot = lax.rem(step, ring)
        return pltpu.make_async_copy(
            up_hbm.at[block(step, depth), :], chunks.at[slot], sems.at[slot]
        )

    def down_copy(step):
        slot = lax.rem(step + up_steps, ring)
        part = down_hbm.at[
            block(lax.rem(step, down_parts), depth), block(lax.div(step, down_parts), width)
        ]
        return pltpu.make_async_copy(part, chunks.at[slot], sems.at[slot])

    def issue(step):
        @pl.when(step < up_steps)
        def _():
            up_copy(step).start()

        @pl.when((step >= up_steps) & (step < up_steps + down_steps))
        def _():
            down_copy(step - up_steps).start()

    for step in range(ring):
        issue(jnp.int32(step))
    at = 0
    for piece in pieces:
        x[at : at + piece.shape[0], :] = piece[...]
        at += piece.shape[0]
    gate_sum[...] = jnp.zeros_like(gate_sum)
    up_sum[...] = jnp.zeros_like(up_sum)

    offset = 0
    for part in gates:
        gate_depth = part.shape[0] // 2

        @pl.loop(0, part.shape[0] // gate_depth)
        def _(step):
            columns = pl.ds(pl.multiple_of(offset + step * gate_depth, 256), gate_depth)
            gate_sum[...] += jnp.dot(
                x[:, columns], part[block(step, gate_depth), :], preferred_element_type=jnp.float32
            )

        offset += part.shape[0]

    @pl.loop(0, up_steps)
    def _(step):
        up_copy(step).wait()
        up_sum[...] += jnp.dot(
            x[:, block(step, depth)], chunks[lax.rem(step, ring)], preferred_element_type=jnp.float32
        )
        issue(step + ring)

    gate_proj = gate_sum[...]
    active[...] = (gate_proj / (1.0 + jnp.exp(-gate_proj)) * up_sum[...]).astype(jnp.bfloat16)

    @pl.loop(0, down_steps // down_parts)
    def _(column):
        for part in range(down_parts):
            step = column * down_parts + part
            down_copy(step).wait()
            out = jnp.dot(
                active[:, part * depth : (part + 1) * depth],
                chunks[lax.rem(step + up_steps, ring)],
                preferred_element_type=jnp.float32,
            )
            if part > 0:
                out += gate_sum[...]
            if part + 1 < down_parts:
                gate_sum[...] = out
            else:
                keep_ref[:, block(column, width)] = out[:half]
                send_ref[:, block(column, width)] = out[half:].astype(jnp.bfloat16)
            issue(step + up_steps + ring)


def expert_ffn(pieces, gates, w_up, w_down):
    rows = sum(piece.shape[0] for piece in pieces)
    model_width, units = w_up.shape
    ring, depth = 9, min(512, units)
    return pl.pallas_call(
        functools.partial(ffn_kernel, len(pieces), len(gates)),
        out_shape=(
            jax.ShapeDtypeStruct((rows // 2, model_width), jnp.float32),
            jax.ShapeDtypeStruct((rows // 2, model_width), jnp.bfloat16),
        ),
        in_specs=[VMEM] * (len(pieces) + len(gates)) + [HBM, HBM],
        out_specs=(VMEM, VMEM),
        scratch_shapes=[
            pltpu.VMEM((ring, depth, units), jnp.bfloat16),
            pltpu.VMEM((rows, model_width), jnp.bfloat16),
            pltpu.VMEM((rows, units), jnp.float32),
            pltpu.VMEM((rows, units), jnp.float32),
            pltpu.VMEM((rows, units), jnp.bfloat16),
            pltpu.SemaphoreType.DMA((ring,)),
        ],
        compiler_params=pltpu.CompilerParams(vmem_limit_bytes=22 * MIB),
        cost_estimate=pl.CostEstimate(
            flops=6 * rows * model_width * units,
            bytes_accessed=6 * model_width * units,
            transcendentals=rows * units,
        ),
    )(*pieces, *gates, w_up, w_down)


def split_kernel(keep_ref, received_ref, *refs):
    kept_ref, sent_refs = refs[-1], refs[-2]
    total = keep_ref[...] + received_ref[...].astype(jnp.float32)
    at = kept_ref.shape[0]
    kept_ref[...] = total[:at]
    sent_refs[...] = total[at:].astype(jnp.bfloat16)


def split_in_two(keep, received):
    half, width = keep.shape[0] // 2, keep.shape[1]
    sent, kept = pl.pallas_call(
        split_kernel,
        in_specs=[VMEM, VMEM],
        out_specs=(VMEM, VMEM),
        out_shape=(
            jax.ShapeDtypeStruct((half, width), jnp.bfloat16),
            jax.ShapeDtypeStruct((half, width), jnp.float32),
        ),
        compiler_params=pltpu.CompilerParams(vmem_limit_bytes=16 * MIB),
    )(keep, received)
    return kept, sent


def split_by_expert_kernel(keep_ref, received_ref, token_ref, kept_ref, *sent_refs):
    total = keep_ref[...] + received_ref[...].astype(jnp.float32)
    rows = kept_ref.shape[0]
    kept_ref[...] = total[:rows]
    for k, sent_ref in enumerate(sent_refs):
        sent_ref[...] = total[(k + 1) * rows : (k + 2) * rows].astype(jnp.bfloat16)


def split_by_expert(keep, received, token):
    rows, width = keep.shape[0] // EXPERTS, keep.shape[1]
    return pl.pallas_call(
        split_by_expert_kernel,
        in_specs=[VMEM, VMEM, VMEM],
        out_specs=(VMEM,) * EXPERTS,
        out_shape=(jax.ShapeDtypeStruct((rows, width), jnp.float32),)
        + (jax.ShapeDtypeStruct((rows, width), jnp.bfloat16),) * (EXPERTS - 1),
        compiler_params=pltpu.CompilerParams(vmem_limit_bytes=16 * MIB),
    )(keep, received, token)


def finish_kernel(hidden_ref, coefficient_ref, kept_ref, *refs):
    received_refs, out_ref = refs[:-1], refs[-1]
    mixture = coefficient_ref[:, 0:1] * kept_ref[...]
    for k, received_ref in enumerate(received_refs):
        mixture += coefficient_ref[:, k + 1 : k + 2] * received_ref[...].astype(jnp.float32)
    out_ref[...] = (hidden_ref[...].astype(jnp.float32) + mixture).astype(jnp.bfloat16)


def finish(hidden, coefficient, kept, received):
    return pl.pallas_call(
        finish_kernel,
        in_specs=[VMEM] * (3 + len(received)),
        out_specs=VMEM,
        out_shape=jax.ShapeDtypeStruct(hidden.shape, jnp.bfloat16),
        compiler_params=pltpu.CompilerParams(vmem_limit_bytes=8 * MIB),
    )(hidden, coefficient, kept, *received)


def attend_kernel(
    lengths_ref, queries_ref, keys_ref, values_ref, context_ref, token_ref,
    query_heads, context_heads,
):
    token_ref[...] = jnp.zeros_like(token_ref)
    row_count, cache_span, width = keys_ref.shape
    group = HEADS // KV_HEADS
    for h in range(HEADS):
        query_heads[:, h, :] = queries_ref[:, h * HEAD_DIM : (h + 1) * HEAD_DIM].astype(jnp.float32)
    own_head = lax.broadcasted_iota(jnp.int32, (HEADS, width), 0) // group
    lane_head = lax.broadcasted_iota(jnp.int32, (HEADS, width), 1) // HEAD_DIM
    on_diagonal = own_head == lane_head
    slot = lax.broadcasted_iota(jnp.int32, (HEADS, cache_span), 1)
    for r in range(row_count):
        spread = jnp.where(on_diagonal, jnp.concatenate([query_heads[r]] * KV_HEADS, axis=1), 0.0)
        scores = lax.dot_general(
            spread.astype(jnp.bfloat16), keys_ref[r], (((1,), (1,)), ((), ())),
            preferred_element_type=jnp.float32,
        ) * HEAD_DIM ** (-0.5)
        scores = jnp.where(slot < lengths_ref[r], scores, -jnp.inf)
        raised = jnp.exp(scores - jnp.max(scores, axis=-1, keepdims=True))
        weights = (raised / jnp.sum(raised, axis=-1, keepdims=True)).astype(jnp.bfloat16)
        mixed = jnp.dot(weights, values_ref[r], preferred_element_type=jnp.float32)
        mixed = jnp.where(on_diagonal, mixed, 0.0)
        folded = mixed[:, :HEAD_DIM]
        for j in range(1, KV_HEADS):
            folded = folded + mixed[:, j * HEAD_DIM : (j + 1) * HEAD_DIM]
        context_heads[r] = folded
    for h in range(HEADS):
        context_ref[:, h * HEAD_DIM : (h + 1) * HEAD_DIM] = context_heads[:, h, :].astype(jnp.bfloat16)


def attend(queries, keys_cache, values_cache, lengths):
    row_count, cache_span, width = keys_cache.shape
    return pl.pallas_call(
        attend_kernel,
        out_shape=(
            jax.ShapeDtypeStruct(queries.shape, jnp.bfloat16),
            jax.ShapeDtypeStruct((8, 128), jnp.float32),
        ),
        in_specs=[SMEM, VMEM, VMEM, VMEM],
        out_specs=(VMEM, VMEM),
        scratch_shapes=[
            pltpu.VMEM((row_count, HEADS, HEAD_DIM), jnp.float32),
            pltpu.VMEM((row_count, HEADS, HEAD_DIM), jnp.float32),
        ],
        compiler_params=pltpu.CompilerParams(vmem_limit_bytes=8 * MIB),
        cost_estimate=pl.CostEstimate(
            flops=4 * row_count * HEADS * cache_span * width,
            bytes_accessed=4 * row_count * cache_span * width,
            transcendentals=row_count * HEADS * cache_span,
        ),
    )(lengths, queries, keys_cache, values_cache)


def local(
    queries,
    keys_cache,
    values_cache,
    lengths,
    hidden,
    norm_gain,
    expert_ids,
    gate_weights,
    w_gate,
    w_up,
    w_down,
):
    devices = lax.axis_size("pool")
    group_size = devices // EXPERTS
    own_rows = hidden.shape[0]

    def swap(value, distance):
        return lax.ppermute(value, "pool", [(i, i ^ distance) for i in range(devices)])

    near = []
    distance = 1
    while distance < group_size:
        near.append(distance)
        distance *= 2

    normed = normalize(hidden, norm_gain)
    first = prefetch([(w_gate, 0, 3584)], normed, 36)
    blocks = [normed] + [swap(normed, k * group_size) for k in range(1, EXPERTS)]
    x = merge(blocks, [first[-1]])
    second = prefetch([(w_gate, 3584, 2560)], x, 24)
    pieces, after = [x], [second[-1]]
    for distance in reversed(near):
        arrived = [swap(piece, distance) for piece in pieces]
        if after:
            arrived[0] = merge(arrived[:1], after)
        pieces, after = pieces + arrived, []
    keep, send = expert_ffn(pieces, first + second, w_up, w_down)

    context, token = attend(queries, keys_cache, values_cache, lengths)
    own_expert = lax.axis_index("pool") // group_size
    order = own_expert ^ jnp.arange(EXPERTS, dtype=jnp.int32)
    named = expert_ids[:, :, None] == order[None, None, :]
    coefficient = jnp.sum(
        jnp.where(named, gate_weights.astype(jnp.float32)[:, :, None], 0.0), axis=1
    )
    for distance in near[:-1]:
        keep, send = split_in_two(keep, swap(send, distance))
    kept, *sent = split_by_expert(keep, swap(send, near[-1]), token)
    received = [swap(block, (k + 1) * group_size) for k, block in enumerate(sent)]
    moe_out = finish(hidden, coefficient, kept, received)
    return (context, moe_out)


def solution(mesh):
    return jax.shard_map(
        local,
        mesh=mesh,
        in_specs=(
            P(("groups", "pool"), None),
            P(("groups", "pool"), None, None),
            P(("groups", "pool"), None, None),
            P(("groups", "pool")),
            P(("groups", "pool"), None),
            P(),
            P(("groups", "pool"), None),
            P(("groups", "pool"), None),
            P(None, "pool"),
            P(None, "pool"),
            P("pool", None),
        ),
        out_specs=(P(("groups", "pool"), None), P(("groups", "pool"), None)),
        check_vma=False,
    )
```
